32 devices in a mesh: ctx: 16 (over z, x, core), tp: 2 (over y).
Axes of the slice: x: 2, y: 2, z: 4, core: 2. Of those that a mesh axis runs over, the one named last changes fastest.
Arguments:
- queries: bfloat16 [2048, 4096], P('ctx', 'tp'), may hold values from -5 to 5
- keys: bfloat16 [2048, 1024], P('ctx', 'tp'), may hold values from -5 to 5
- values: bfloat16 [2048, 1024], P('ctx', 'tp'), may hold values from -6 to 6
- docs: int32 [2048], P('ctx'), may hold values from 0 to 11, never falling along the last dimension, each value on 1 to 1152 neighbouring positions
- out_weight: bfloat16 [4096, 4096], P('tp'), may hold values from -0.09375 to 0.09375
Outputs:
- mixed: bfloat16 [2048, 4096], P('ctx', 'tp')
The draws below stay inside these ranges and needn't reach their ends.
All inputs are finite; a program needn't handle non-finite values.
Results may differ from the reference program's by a relative error of at most 0.014.
Values may be sent and summed in bfloat16 or wider, within the bound.
A program may use at most 64 MiB of HBM per device.

```python
import math
import jax
import jax.numpy as jnp
import numpy as np
from jax import lax

D = 4096
HEADS = 32
KV_HEADS = 8
HEAD_DIM = 128
TOK_DEV = 128
DOCS = 12
TOKENS = 2048


def draw_keys(key, part):
    shape = (TOKENS, KV_HEADS * HEAD_DIM)
    base = jnp.clip(1.7 * jax.random.normal(jax.random.fold_in(key, 11), shape, jnp.float32), -5.0, 5.0)
    return base.astype(jnp.bfloat16)


def draw_queries(key, part):
    shape = (TOKENS, HEADS * HEAD_DIM)
    base = jnp.clip(1.7 * jax.random.normal(jax.random.fold_in(key, 13), shape, jnp.float32), -5.0, 5.0)
    return base.astype(jnp.bfloat16)


def block_levels(stream_key, dims, pieces, low, top_value):
    def one(position, shards_of):
        draws = jax.random.uniform(jax.random.fold_in(jax.random.fold_in(stream_key, 6), position), (shards_of,), jnp.float32, low / len(pieces), top_value / len(pieces))
        return jnp.repeat(jnp.exp(draws), dims[position] // shards_of).reshape((-1,) + (1,) * (len(dims) - position - 1))

    factor_of = one(*pieces[0])
    for cut in pieces[1:]:
        factor_of = factor_of * one(*cut)
    return factor_of


def length_profile(count, total, bound, skew):
    loads = [(1 << 20) // math.isqrt(rank ** skew) + 1 for rank in range(2, count + 1)]
    surplus, given = total - bound - (count - 1), [1] * (count - 1)
    while surplus > 0:
        movable = [i for i in range(count - 1) if given[i] < bound]
        pool, left = sum([loads[i] for i in movable]), surplus
        for i in movable:
            addition = min(bound - given[i], max(1, left * loads[i] // pool), surplus)
            given[i] = given[i] + addition
            surplus = surplus - addition
    return np.array([bound] + given)


def ragged(key, number_of, total, limit, slope):
    if number_of == 2:
        one = jax.random.randint(key, (), max(1, total - limit), min(limit, total - 1) + 1)
        return jnp.stack([one, total - one])
    lengths = jnp.asarray(length_profile(number_of, total, limit, slope), jnp.int32)
    pairs = (number_of - 1) // 2
    giver, receiver = lengths[1:1 + 2 * pairs:2], lengths[2:2 + 2 * pairs:2]
    room = jnp.minimum(giver - 1, limit - receiver)
    moved = jax.random.randint(jax.random.fold_in(key, 1), (pairs,), 0, 1 << 20) % (room + 1)
    lengths = lengths.at[1:1 + 2 * pairs:2].set(giver - moved).at[2:2 + 2 * pairs:2].set(receiver + moved)
    return lengths[jax.random.permutation(jax.random.fold_in(key, 2), number_of)]


def scatter_about(stream_key, shape, scale, most, split=(), kind=jnp.bfloat16):
    values = scale * jax.random.normal(stream_key, shape, jnp.float32)
    if split:
        values = values * block_levels(stream_key, shape, split, -0.22, 0.18)
    return jnp.clip(values, -most, most).astype(kind)


def setup_inputs(seed: int = 0) -> dict:
    key_list = jax.random.split(jax.random.key(seed), 6)
    return {
        "queries": draw_queries(jax.random.fold_in(key_list[5], 71), 0),
        "keys": draw_keys(jax.random.fold_in(key_list[5], 71), 0),
        "values": scatter_about(key_list[2], (TOKENS, KV_HEADS * HEAD_DIM), 1.0, 6.0, ((0, 16), (1, 2))),
        "docs": jnp.searchsorted(jnp.cumsum(ragged(key_list[3], DOCS, TOKENS, TOKENS // 2 + TOK_DEV, 2)), jnp.arange(TOKENS), side="right").astype(jnp.int32),
        "out_weight": scatter_about(key_list[4], (HEADS * HEAD_DIM, D), (HEADS * HEAD_DIM) ** -0.5, 0.09375, ((0, 2),)),
    }


def reference(queries, keys, values, docs, out_weight):
    group_size = HEADS // KV_HEADS
    scale = 1.0 / math.sqrt(HEAD_DIM)
    key_float = keys.astype(jnp.float32).reshape(TOKENS, KV_HEADS, HEAD_DIM)
    value_float = values.astype(jnp.float32).reshape(TOKENS, KV_HEADS, HEAD_DIM)
    columns = jnp.arange(TOKENS, dtype=jnp.int32)

    def block(index):
        start = index * TOK_DEV
        query_block = lax.dynamic_slice_in_dim(queries, start, TOK_DEV, 0)
        query_block = query_block.astype(jnp.float32).reshape(TOK_DEV, KV_HEADS, group_size, HEAD_DIM)
        doc_block = lax.dynamic_slice_in_dim(docs, start, TOK_DEV, 0)
        row_positions = start + jnp.arange(TOK_DEV, dtype=jnp.int32)
        scores = jnp.einsum('igkd,jgd->gkij', query_block, key_float) * scale
        allowed = (columns[None, :] <= row_positions[:, None]) & (docs[None, :] == doc_block[:, None])
        peak = lax.optimization_barrier(jnp.max(jnp.where(allowed, scores, -1e+30), axis=-1, keepdims=True))
        weight = jnp.where(allowed, jnp.exp(scores - peak), 0.0)
        total = lax.optimization_barrier(jnp.sum(weight, axis=-1))
        rounded = lax.optimization_barrier(weight.astype(jnp.bfloat16)).astype(jnp.float32)
        summed = jnp.einsum('gkij,jgd->gkid', rounded, value_float) / total[..., None]
        summed = jnp.transpose(summed, (2, 0, 1, 3)).reshape(TOK_DEV, HEADS * HEAD_DIM)
        return summed.astype(jnp.bfloat16)
    attention = lax.map(block, jnp.arange(TOKENS // TOK_DEV, dtype=jnp.int32))
    attention = attention.reshape(TOKENS, HEADS * HEAD_DIM)
    return jnp.dot(attention, out_weight, preferred_element_type=jnp.float32).astype(jnp.bfloat16)
```

```python
import functools
import math

import jax
import jax.numpy as jnp
from jax import lax
from jax.experimental import pallas as pl
from jax.experimental.pallas import tpu as pltpu
from jax.sharding import PartitionSpec as P

HEAD_DIM = 128
LEVEL = 4
MESH = pl.DeviceIdType.MESH


def both(*terms):
    out = terms[0]
    for term in terms[1:]:
        out = jnp.logical_and(out, term)
    return out


def kernel(
    n_ctx, n_tp, far, cw,
    q_ref, doc_ref, k_hbm, v_hbm, w_hbm, out_ref,
    kv, docs, w_vmem, attn, outgoing, incoming, bias,
    stage_sem, w_sem, recv_sem, up_sem, x_sem, core_sem, hop_sem,
    doc_send, doc_recv, tp_send, tp_recv,
):
    rows = q_ref.shape[0]
    kv_heads = k_hbm.shape[1] // HEAD_DIM
    group = q_ref.shape[1] // k_hbm.shape[1]
    levels = n_ctx // LEVEL
    top = (far + LEVEL - 1) // LEVEL
    count = far + 1
    cols = out_ref.shape[1]
    chunks = cols // cw

    me = lax.axis_index("ctx")
    t = lax.axis_index("tp")
    z, r = me // LEVEL, me % LEVEL
    r1 = r + 1 - 2 * (r % 2)
    r2 = (r + 2) % LEVEL
    r3 = LEVEL - 1 - r
    base = me - r

    def needs(k, reader, owner):
        gap = LEVEL * k + reader - owner
        return both(z >= k, gap >= 0, gap <= far)

    def either(a, b):
        return jnp.logical_or(a, b)

    own = LEVEL - 1 - r
    staged = []
    for h in range(kv_heads):
        span = slice(h * HEAD_DIM, (h + 1) * HEAD_DIM)
        for i, src in enumerate((k_hbm, v_hbm)):
            c = pltpu.make_async_copy(src.at[:, span], kv.at[own, h, i], stage_sem.at[h, i])
            c.start()
            staged.append(c)

    barrier = pltpu.get_barrier_semaphore()

    def greet(device):
        pl.semaphore_signal(barrier, inc=1, device_id=device, device_id_type=MESH)

    for d in range(1, far + 1):
        @pl.when(me - d >= 0)
        def _():
            greet({"ctx": me - d})
    for other in (r1, r2):
        @pl.when(other > r)
        def _():
            greet({"ctx": base + other})
    for dt in range(1, n_tp):
        greet({"tp": (t + dt) % n_tp})
    waits = jnp.minimum(far, n_ctx - 1 - me) + (n_tp - 1)
    waits = waits + jnp.where(r1 < r, 1, 0) + jnp.where(r2 < r, 1, 0)
    pl.semaphore_wait(barrier, waits)

    docs[0] = doc_ref[...]

    def doc_copy(d):
        return pltpu.make_async_remote_copy(
            src_ref=doc_ref, dst_ref=docs.at[d], send_sem=doc_send.at[d], recv_sem=doc_recv.at[d],
            device_id={"ctx": me + d}, device_id_type=MESH)

    for d in range(1, far + 1):
        @pl.when(me + d < n_ctx)
        def _():
            doc_copy(d).start()

    def copy(src_slot, dst_slot, h, send, device):
        return pltpu.make_async_remote_copy(
            src_ref=kv.at[src_slot, h], dst_ref=kv.at[dst_slot, h],
            send_sem=send, recv_sem=recv_sem.at[dst_slot, h],
            device_id={"ctx": device}, device_id_type=MESH)

    def slot(k, owner):
        return LEVEL * k + LEVEL - 1 - owner

    def up(k, h):
        return copy(slot(k, r), slot(k + 1, r), h, up_sem.at[k, h], me + LEVEL)

    def across(k, h):
        return copy(slot(k, r), slot(k, r), h, x_sem.at[k, h], base + r2)

    def core(k, h):
        return copy(slot(k, r), slot(k, r), h, core_sem.at[k, h], base + r1)

    def hop(k, h):
        return copy(slot(k, r2), slot(k, r2), h, hop_sem.at[k, h], base + r1)

    def goes_up(k):
        return both(z >= k, z + 1 < levels, LEVEL * (k + 1) - r <= far)

    def goes_across(k):
        return either(needs(k, r2, r), needs(k, r3, r))

    def arrived(where, h):
        pltpu.make_async_copy(kv.at[where, h], kv.at[where, h], recv_sem.at[where, h]).wait()

    def column(k, h):
        if k > 0:
            @pl.when(both(z >= k, LEVEL * k - r <= far))
            def _():
                arrived(slot(k, r), h)

        @pl.when(goes_up(k))
        def _():
            up(k, h).start()

        @pl.when(goes_across(k))
        def _():
            across(k, h).start()

        @pl.when(needs(k, r1, r))
        def _():
            core(k, h).start()

    def crossed(k, h):
        @pl.when(either(needs(k, r, r2), needs(k, r1, r2)))
        def _():
            arrived(slot(k, r2), h)

        @pl.when(needs(k, r1, r2))
        def _():
            hop(k, h).start()

    def rest(k, h):
        for owner in (r1, r3):
            @pl.when(needs(k, r, owner))
            def _():
                arrived(slot(k, owner), h)

    def own_sends(h):
        staged[2 * h].wait()
        staged[2 * h + 1].wait()
        column(0, h)

    for h in range(min(2, kv_heads)):
        own_sends(h)

    w_copy = pltpu.make_async_copy(w_hbm, w_vmem, w_sem)
    w_copy.start()

    for u in range(LEVEL, kv.shape[0]):
        @pl.when(u > LEVEL * z + LEVEL - 1)
        def _():
            kv[u] = jnp.zeros(kv.shape[1:], kv.dtype)

    for d in range(1, far + 1):
        @pl.when(d > me)
        def _():
            docs[d] = jnp.full(docs.shape[1:], 1 << 30, docs.dtype)

        @pl.when(me >= d)
        def _():
            pltpu.make_async_copy(docs.at[d], docs.at[d], doc_recv.at[d]).wait()

    doc_column = jnp.transpose(jnp.broadcast_to(docs[0], (rows, rows)))
    smaller = jnp.zeros((rows, rows), jnp.int32)
    for d in range(far + 1):
        smaller = smaller + jnp.where(docs[d] < doc_column, 1, 0)
    start = jnp.sum(smaller, axis=1, keepdims=True)
    start = start + rows * jnp.maximum(me - far, 0)
    ahead = lax.broadcasted_iota(jnp.int32, (rows, rows), 1)
    position = lax.broadcasted_iota(jnp.int32, (rows, rows), 0)
    bias[0] = jnp.where((me * rows + ahead >= start) & (ahead <= position), 0.0, -1e30)
    for d in range(1, count):
        bias[d] = jnp.where((me - d) * rows + ahead >= start, 0.0, -1e30)

    scale = math.log2(math.e) / math.sqrt(HEAD_DIM)

    def attend(h, g):
        head = h * group + g
        span = slice(head * HEAD_DIM, (head + 1) * HEAD_DIM)
        query = q_ref[:, span]
        parts = []
        for d in range(count):
            s = lax.dot_general(query, kv[own + d, h, 0], (((1,), (1,)), ((), ())),
                                preferred_element_type=jnp.float32)
            parts.append(s + bias[d])
        scores = jnp.concatenate(parts, axis=1)
        peak = jnp.max(scores, axis=1, keepdims=True)
        weight = jnp.exp2((scores - peak) * scale)
        total = jnp.sum(weight, axis=1, keepdims=True)
        values = jnp.concatenate([kv[own + d, h, 1] for d in range(count)], axis=0)
        summed = jnp.dot(weight.astype(jnp.bfloat16), values, preferred_element_type=jnp.float32)
        attn[:, span] = (summed / total).astype(jnp.bfloat16)

    def service(h):
        steps = []
        if h + 1 < kv_heads and h > 0:
            steps.append(functools.partial(own_sends, h + 1))
        for k in range(1, top + 2):
            if k <= top:
                steps.append(functools.partial(column, k, h))
            steps.append(functools.partial(crossed, k - 1, h))
        return steps

    for h in range(kv_heads + 1):
        steps = service(h) if h < kv_heads else []
        if h == 0:
            for step in steps:
                step()
            continue
        for k in range(top + 1):
            rest(k, h - 1)
        per = -(-len(steps) // group)
        for g in range(group):
            attend(h - 1, g)
            for step in steps[g * per:(g + 1) * per]:
                step()

    w_copy.wait()

    def tp_copy(dt, c):
        return pltpu.make_async_remote_copy(
            src_ref=outgoing.at[dt - 1, c], dst_ref=incoming.at[dt - 1, c],
            send_sem=tp_send.at[dt - 1, c], recv_sem=tp_recv.at[dt - 1, c],
            device_id={"tp": (t + dt) % n_tp}, device_id_type=MESH)

    def project(owner, c):
        at = pl.multiple_of(owner * cols + c * cw, cw)
        return jnp.dot(attn[...], w_vmem[:, pl.ds(at, cw)], preferred_element_type=jnp.float32)

    for dt in range(1, n_tp):
        @pl.loop(0, chunks)
        def _(c):
            outgoing[dt - 1, c] = project((t + dt) % n_tp, c).astype(jnp.bfloat16)
            tp_copy(dt, c).start()

    @pl.loop(0, chunks)
    def _(c):
        total = project(t, c)
        for dt in range(1, n_tp):
            tp_copy(dt, c).wait_recv()
            total = total + incoming[dt - 1, c].astype(jnp.float32)
        out_ref[:, pl.ds(pl.multiple_of(c * cw, cw), cw)] = total.astype(out_ref.dtype)

    for dt in range(1, n_tp):
        @pl.loop(0, chunks)
        def _(c):
            tp_copy(dt, c).wait_send()
    for d in range(1, far + 1):
        @pl.when(me + d < n_ctx)
        def _():
            doc_copy(d).wait_send()
    for k in range(top + 1):
        for cond, make in ((goes_up(k), up), (goes_across(k), across),
                           (needs(k, r1, r), core), (needs(k, r1, r2), hop)):
            @pl.when(cond)
            def _():
                for h in range(kv_heads):
                    make(k, h).wait_send()


def shards(n_ctx, n_tp, queries, keys, values, docs, out_weight):
    rows = queries.shape[0]
    tokens = rows * n_ctx
    longest = tokens // 2 + rows
    far = min(n_ctx - 1, (longest - 1 + rows - 1) // rows)
    kv_heads = keys.shape[1] // HEAD_DIM
    top = (far + LEVEL - 1) // LEVEL
    slots = far + LEVEL
    cols = out_weight.shape[1] // n_tp
    cw = min(256, cols)
    chunks = cols // cw
    dma = pltpu.SemaphoreType.DMA
    anywhere = pl.BlockSpec(memory_space=pl.ANY)
    vmem = pl.BlockSpec(memory_space=pltpu.VMEM)
    return pl.pallas_call(
        functools.partial(kernel, n_ctx, n_tp, far, cw),
        out_shape=jax.ShapeDtypeStruct((rows, cols), jnp.bfloat16),
        in_specs=[vmem, vmem, anywhere, anywhere, anywhere],
        out_specs=vmem,
        scratch_shapes=[
            pltpu.VMEM((slots, kv_heads, 2, rows, HEAD_DIM), jnp.bfloat16),
            pltpu.VMEM((far + 1, 1, rows), jnp.int32),
            pltpu.VMEM(out_weight.shape, jnp.bfloat16),
            pltpu.VMEM(queries.shape, jnp.bfloat16),
            pltpu.VMEM((n_tp - 1, chunks, rows, cw), jnp.bfloat16),
            pltpu.VMEM((n_tp - 1, chunks, rows, cw), jnp.bfloat16),
            pltpu.VMEM((far + 1, rows, rows), jnp.float32),
            dma((kv_heads, 2)),
            dma,
            dma((slots, kv_heads)),
            dma((top + 1, kv_heads)),
            dma((top + 1, kv_heads)),
            dma((top + 1, kv_heads)),
            dma((top + 1, kv_heads)),
            dma((far + 1,)),
            dma((far + 1,)),
            dma((n_tp - 1, chunks)),
            dma((n_tp - 1, chunks)),
        ],
        compiler_params=pltpu.CompilerParams(
            collective_id=0, has_side_effects=True, vmem_limit_bytes=56 * 1024 * 1024
        ),
    )(queries, docs.reshape(1, rows), keys, values, out_weight)


def solution(mesh):
    placed = (P("ctx", "tp"), P("ctx", "tp"), P("ctx", "tp"), P("ctx"), P("tp", None))
    return jax.shard_map(
        functools.partial(shards, mesh.shape["ctx"], mesh.shape["tp"]),
        mesh=mesh, in_specs=placed, out_specs=P("ctx", "tp"), check_vma=False,
    )
```

```python
import functools
import math

import jax
import jax.numpy as jnp
from jax import lax
from jax.experimental import pallas as pl
from jax.experimental.pallas import tpu as pltpu
from jax.sharding import PartitionSpec as P

HEAD_DIM = 128
LEVEL = 4
MESH = pl.DeviceIdType.MESH


def both(*terms):
    out = terms[0]
    for term in terms[1:]:
        out = jnp.logical_and(out, term)
    return out


def kernel(
    n_ctx, n_tp, far, cw,
    q_hbm, doc_ref, k_hbm, v_hbm, w_hbm, out_ref,
    kv, docs, q_ref, w_vmem, attn, outgoing, incoming, bias, held, peaks,
    stage_sem, q_sem, w_sem, recv_sem, up_sem, x_sem, core_sem, hop_sem,
    doc_send, doc_recv, tp_send, tp_recv,
):
    rows = q_hbm.shape[0]
    kv_heads = k_hbm.shape[1] // HEAD_DIM
    group = q_hbm.shape[1] // k_hbm.shape[1]
    levels = n_ctx // LEVEL
    top = (far + LEVEL - 1) // LEVEL
    count = far + 1
    cols = out_ref.shape[1]
    chunks = cols // cw

    me = lax.axis_index("ctx")
    t = lax.axis_index("tp")
    z, r = me // LEVEL, me % LEVEL
    r1 = r + 1 - 2 * (r % 2)
    r2 = (r + 2) % LEVEL
    r3 = LEVEL - 1 - r
    base = me - r

    def needs(k, reader, owner):
        gap = LEVEL * k + reader - owner
        return both(z >= k, gap >= 0, gap <= far)

    def either(a, b):
        return jnp.logical_or(a, b)

    own = LEVEL - 1 - r
    staged = []
    for h in range(kv_heads):
        span = slice(h * HEAD_DIM, (h + 1) * HEAD_DIM)
        for i, src in enumerate((k_hbm, v_hbm)):
            c = pltpu.make_async_copy(src.at[:, span], kv.at[own, h, i], stage_sem.at[h, i])
            c.start()
            staged.append(c)
    q_copy = pltpu.make_async_copy(q_hbm, q_ref, q_sem)
    q_copy.start()

    barrier = pltpu.get_barrier_semaphore()

    def greet(device):
        pl.semaphore_signal(barrier, inc=1, device_id=device, device_id_type=MESH)

    for d in range(1, far + 1):
        @pl.when(me - d >= 0)
        def _():
            greet({"ctx": me - d})
    for other in (r1, r2):
        @pl.when(other > r)
        def _():
            greet({"ctx": base + other})
    for dt in range(1, n_tp):
        greet({"tp": (t + dt) % n_tp})
    waits = jnp.minimum(far, n_ctx - 1 - me) + (n_tp - 1)
    waits = waits + jnp.where(r1 < r, 1, 0) + jnp.where(r2 < r, 1, 0)
    pl.semaphore_wait(barrier, waits)

    docs[0] = doc_ref[...]

    def doc_copy(d):
        return pltpu.make_async_remote_copy(
            src_ref=doc_ref, dst_ref=docs.at[d], send_sem=doc_send.at[d], recv_sem=doc_recv.at[d],
            device_id={"ctx": me + d}, device_id_type=MESH)

    for d in range(1, far + 1):
        @pl.when(me + d < n_ctx)
        def _():
            doc_copy(d).start()

    def copy(src_slot, dst_slot, h, send, device):
        return pltpu.make_async_remote_copy(
            src_ref=kv.at[src_slot, h], dst_ref=kv.at[dst_slot, h],
            send_sem=send, recv_sem=recv_sem.at[dst_slot, h],
            device_id={"ctx": device}, device_id_type=MESH)

    def slot(k, owner):
        return LEVEL * k + LEVEL - 1 - owner

    def up(k, h):
        return copy(slot(k, r), slot(k + 1, r), h, up_sem.at[k, h], me + LEVEL)

    def across(k, h):
        return copy(slot(k, r), slot(k, r), h, x_sem.at[k, h], base + r2)

    def core(k, h):
        return copy(slot(k, r), slot(k, r), h, core_sem.at[k, h], base + r1)

    def hop(k, h):
        return copy(slot(k, r2), slot(k, r2), h, hop_sem.at[k, h], base + r1)

    def goes_up(k):
        return both(z >= k, z + 1 < levels, LEVEL * (k + 1) - r <= far)

    def goes_across(k):
        return either(needs(k, r2, r), needs(k, r3, r))

    def arrived(where, h):
        pltpu.make_async_copy(kv.at[where, h], kv.at[where, h], recv_sem.at[where, h]).wait()

    def column(k, h):
        if k > 0:
            @pl.when(both(z >= k, LEVEL * k - r <= far))
            def _():
                arrived(slot(k, r), h)

        @pl.when(goes_up(k))
        def _():
            up(k, h).start()

        @pl.when(goes_across(k))
        def _():
            across(k, h).start()

        @pl.when(needs(k, r1, r))
        def _():
            core(k, h).start()

    def crossed(k, h):
        @pl.when(either(needs(k, r, r2), needs(k, r1, r2)))
        def _():
            arrived(slot(k, r2), h)

        @pl.when(needs(k, r1, r2))
        def _():
            hop(k, h).start()

    def rest(first, last, h):
        for k in range(first, last + 1):
            for owner in (r1, r3):
                @pl.when(needs(k, r, owner))
                def _():
                    arrived(slot(k, owner), h)

    for h in range(kv_heads):
        staged[2 * h].wait()
        staged[2 * h + 1].wait()
        column(0, h)

    w_copy = pltpu.make_async_copy(w_hbm, w_vmem, w_sem)
    w_copy.start()

    for u in range(LEVEL, kv.shape[0]):
        @pl.when(u > LEVEL * z + LEVEL - 1)
        def _():
            kv[u] = jnp.zeros(kv.shape[1:], kv.dtype)

    for d in range(1, far + 1):
        @pl.when(d > me)
        def _():
            docs[d] = jnp.full(docs.shape[1:], 1 << 30, docs.dtype)

        @pl.when(me >= d)
        def _():
            pltpu.make_async_copy(docs.at[d], docs.at[d], doc_recv.at[d]).wait()

    doc_column = jnp.transpose(jnp.broadcast_to(docs[0], (rows, rows)))
    smaller = jnp.zeros((rows, rows), jnp.int32)
    for d in range(far + 1):
        smaller = smaller + jnp.where(docs[d] < doc_column, 1, 0)
    start = jnp.sum(smaller, axis=1, keepdims=True)
    start = start + rows * jnp.maximum(me - far, 0)
    ahead = lax.broadcasted_iota(jnp.int32, (rows, rows), 1)
    position = lax.broadcasted_iota(jnp.int32, (rows, rows), 0)
    bias[:, :rows] = jnp.where((me * rows + ahead >= start) & (ahead <= position), 0.0, -1e30)
    for d in range(1, count):
        bias[:, d * rows:(d + 1) * rows] = jnp.where((me - d) * rows + ahead >= start, 0.0, -1e30)

    scale = math.log2(math.e) / math.sqrt(HEAD_DIM)

    def attend(h, first, blocks, begin, end):
        heads = range(h * group + first, h * group + first + batch)
        wide = batch * rows
        at = pl.ds(first * rows, wide)
        query = jnp.concatenate(
            [q_ref[:, e * HEAD_DIM:(e + 1) * HEAD_DIM] for e in heads], axis=0)
        keys = jnp.concatenate([kv[own + d, h, 0] for d in blocks], axis=0)
        values = jnp.concatenate([kv[own + d, h, 1] for d in blocks], axis=0)
        values = jnp.concatenate([values, jnp.ones_like(values)], axis=1)
        scores = lax.dot_general(query, keys, (((1,), (1,)), ((), ())),
                                 preferred_element_type=jnp.float32)
        mask = bias[:, blocks[0] * rows:(blocks[-1] + 1) * rows]
        scores = (scores.reshape(batch, rows, -1) + mask[None]).reshape(wide, -1)
        peak = jnp.max(scores, axis=1, keepdims=True)
        if not begin:
            earlier = peaks[h, at]
            peak = jnp.maximum(peak, earlier)
            rescale = jnp.exp2((earlier - peak) * scale)
        weight = jnp.exp2((scores - peak) * scale).astype(jnp.bfloat16)
        summed = jnp.dot(weight, values, preferred_element_type=jnp.float32)
        if not begin:
            summed = summed + held[h, at] * rescale
        if end:
            result = summed[:, :HEAD_DIM] / summed[:, HEAD_DIM:]
            for i, e in enumerate(heads):
                attn[:, e * HEAD_DIM:(e + 1) * HEAD_DIM] = (
                    result[i * rows:(i + 1) * rows].astype(jnp.bfloat16))
        else:
            peaks[h, at] = peak
            held[h, at] = summed

    near = top // 2
    split = LEVEL * near + 1
    batch = 2
    q_copy.wait()
    for k in range(1, top + 1):
        for h in range(kv_heads):
            column(k, h)
            crossed(k - 1, h)
            if k == near + 1:
                rest(0, near, h)
                for g in range(0, group, batch):
                    attend(h, g, range(split), True, split == count)
            if k == top:
                crossed(k, h)
                rest(near + 1, top, h)
                for g in range(0, group, batch):
                    attend(h, g, range(split, count), False, True)

    w_copy.wait()

    def tp_copy(dt, c):
        return pltpu.make_async_remote_copy(
            src_ref=outgoing.at[dt - 1, c], dst_ref=incoming.at[dt - 1, c],
            send_sem=tp_send.at[dt - 1, c], recv_sem=tp_recv.at[dt - 1, c],
            device_id={"tp": (t + dt) % n_tp}, device_id_type=MESH)

    def project(owner, c):
        at = pl.multiple_of(owner * cols + c * cw, cw)
        return jnp.dot(attn[...], w_vmem[:, pl.ds(at, cw)], preferred_element_type=jnp.float32)

    for dt in range(1, n_tp):
        @pl.loop(0, chunks)
        def _(c):
            outgoing[dt - 1, c] = project((t + dt) % n_tp, c).astype(jnp.bfloat16)
            tp_copy(dt, c).start()

    @pl.loop(0, chunks)
    def _(c):
        total = project(t, c)
        for dt in range(1, n_tp):
            tp_copy(dt, c).wait_recv()
            total = total + incoming[dt - 1, c].astype(jnp.float32)
        out_ref[:, pl.ds(pl.multiple_of(c * cw, cw), cw)] = total.astype(out_ref.dtype)

    for dt in range(1, n_tp):
        @pl.loop(0, chunks)
        def _(c):
            tp_copy(dt, c).wait_send()
    for d in range(1, far + 1):
        @pl.when(me + d < n_ctx)
        def _():
            doc_copy(d).wait_send()
    for k in range(top + 1):
        for cond, make in ((goes_up(k), up), (goes_across(k), across),
                           (needs(k, r1, r), core), (needs(k, r1, r2), hop)):
            @pl.when(cond)
            def _():
                for h in range(kv_heads):
                    make(k, h).wait_send()


def shards(n_ctx, n_tp, queries, keys, values, docs, out_weight):
    rows = queries.shape[0]
    tokens = rows * n_ctx
    longest = tokens // 2 + rows
    far = min(n_ctx - 1, (longest - 1 + rows - 1) // rows)
    kv_heads = keys.shape[1] // HEAD_DIM
    group = queries.shape[1] // keys.shape[1]
    top = (far + LEVEL - 1) // LEVEL
    slots = far + LEVEL
    cols = out_weight.shape[1] // n_tp
    cw = min(256, cols)
    chunks = cols // cw
    dma = pltpu.SemaphoreType.DMA
    anywhere = pl.BlockSpec(memory_space=pl.ANY)
    vmem = pl.BlockSpec(memory_space=pltpu.VMEM)
    return pl.pallas_call(
        functools.partial(kernel, n_ctx, n_tp, far, cw),
        out_shape=jax.ShapeDtypeStruct((rows, cols), jnp.bfloat16),
        in_specs=[anywhere, vmem, anywhere, anywhere, anywhere],
        out_specs=vmem,
        scratch_shapes=[
            pltpu.VMEM((slots, kv_heads, 2, rows, HEAD_DIM), jnp.bfloat16),
            pltpu.VMEM((far + 1, 1, rows), jnp.int32),
            pltpu.VMEM(queries.shape, jnp.bfloat16),
            pltpu.VMEM(out_weight.shape, jnp.bfloat16),
            pltpu.VMEM(queries.shape, jnp.bfloat16),
            pltpu.VMEM((n_tp - 1, chunks, rows, cw), jnp.bfloat16),
            pltpu.VMEM((n_tp - 1, chunks, rows, cw), jnp.bfloat16),
            pltpu.VMEM((rows, (far + 1) * rows), jnp.float32),
            pltpu.VMEM((kv_heads, group * rows, 2 * HEAD_DIM), jnp.float32),
            pltpu.VMEM((kv_heads, group * rows, 1), jnp.float32),
            dma((kv_heads, 2)),
            dma,
            dma,
            dma((slots, kv_heads)),
            dma((top + 1, kv_heads)),
            dma((top + 1, kv_heads)),
            dma((top + 1, kv_heads)),
            dma((top + 1, kv_heads)),
            dma((far + 1,)),
            dma((far + 1,)),
            dma((n_tp - 1, chunks)),
            dma((n_tp - 1, chunks)),
        ],
        compiler_params=pltpu.CompilerParams(
            collective_id=0, has_side_effects=True, vmem_limit_bytes=56 * 1024 * 1024
        ),
    )(queries, docs.reshape(1, rows), keys, values, out_weight)


def solution(mesh):
    placed = (P("ctx", "tp"), P("ctx", "tp"), P("ctx", "tp"), P("ctx"), P("tp", None))
    return jax.shard_map(
        functools.partial(shards, mesh.shape["ctx"], mesh.shape["tp"]),
        mesh=mesh, in_specs=placed, out_specs=P("ctx", "tp"), check_vma=False,
    )
```
